768 devices in a mesh: section: 16 (over y_hi, x, core), fsdp: 48 (over z, y_lo).
Axes of the slice: x: 4, y: 8 (y_hi: 2, y_lo: 4; y = y_hi * 4 + y_lo), z: 12, core: 2. Of those that a mesh axis runs over, the one named last changes fastest.
Arguments:
- saved_input: bfloat16 [16, 2, 256, 6144], P('section', None, None, 'fsdp'), may hold values from -6 to 6
- incoming: bfloat16 [16, 256, 6144], P('section', None, 'fsdp'), may hold values from -6 to 6
- earlier_grad: bfloat16 [16, 256, 6144], P('section', None, 'fsdp'), may hold values from -6 to 6
- w_out: bfloat16 [16, 6144, 6144], P('section', 'fsdp'), may hold values from -0.078125 to 0.078125
- kernel: float32 [16, 3, 6144], P('section', None, 'fsdp'), may hold values from -3.5 to 3.5
- dilation: int32 [16], P('section'), may hold values from 1 to 64
Outputs:
- grad_input: bfloat16 [16, 256, 6144], P('section', None, 'fsdp')
- grad_kernel: float32 [16, 3, 6144], P('section', None, 'fsdp')
- grad_w_out: bfloat16 [16, 6144, 6144], P('section', 'fsdp')
The draws below stay inside these ranges and needn't reach their ends.
All inputs are finite; a program needn't handle non-finite values.
Results may differ from the reference program's by a relative error of at most 0.0049.
Values may be sent and summed in bfloat16 or wider, within the bound.
No kernel may reach another device: no remote copies, remote signals or barrier semaphores. Data moves between devices by JAX's collectives and lax.ppermute only.
A program may use at most 32 MiB of HBM per device.

```python
import jax
import jax.numpy as jnp
from jax import lax

D = 6144
SEQ = 256
TAPS = 3
SECTIONS = 16


def place_ends(drawn, stream_key, low, largest):
    dims = drawn.shape
    spot = [jax.random.randint(jax.random.fold_in(stream_key, axis), (), 0, dims[axis]) for axis in range(len(dims))]
    drawn = drawn.at[tuple(spot)].set(low)
    longest = dims.index(max(dims))
    spot[longest] = (spot[longest] + 1) % dims[longest]
    return drawn.at[tuple(spot)].set(largest)


def levels(key, shape, cuts, least, high):
    level, own = 1.0, jax.random.fold_in(key, 6)
    for axis_at, blocks in cuts:
        draws = jnp.exp(jax.random.uniform(jax.random.fold_in(own, axis_at), (blocks,), jnp.float32, least / len(cuts), high / len(cuts)))
        level = level * jnp.repeat(draws, shape[axis_at] // blocks).reshape([-1 if axis == axis_at else 1 for axis in range(len(shape))])
    return level


def normal_values(own_key, dims, width, limit, shards=(), dtype=jnp.bfloat16):
    array = width * jax.random.normal(own_key, dims, jnp.float32)
    if shards:
        array = array * levels(own_key, dims, shards, -0.22, 0.18)
    return jnp.clip(array, -limit, limit).astype(dtype)


def setup_inputs(seed: int = 0) -> dict:
    key_of = jax.random.split(jax.random.key(seed), 7)
    return {
        "saved_input": normal_values(key_of[0], (SECTIONS, 2, SEQ, D), 1.0, 6.0, ((0, 16), (3, 48))),
        "incoming": normal_values(key_of[1], (SECTIONS, SEQ, D), 1.0, 6.0, ((0, 16), (2, 48))),
        "earlier_grad": normal_values(key_of[2], (SECTIONS, SEQ, D), 1.0, 6.0, ((0, 16), (2, 48))),
        "w_out": normal_values(key_of[3], (SECTIONS, D, D), D ** -0.5, 0.078125, ((0, 16), (1, 48))),
        "kernel": normal_values(key_of[4], (SECTIONS, TAPS, D), TAPS ** -0.5, 3.5, ((0, 16), (2, 48)), jnp.float32),
        "dilation": place_ends(jax.random.randint(key_of[5], (SECTIONS,), 1, SEQ // 4 + 1), jax.random.fold_in(key_of[5], 1), 1, (SEQ // 4 + 1) - 1).astype(jnp.int32),
    }


def delayed(values, offset):
    length = values.shape[-2]
    padded = jnp.concatenate([jnp.zeros_like(values), values], axis=-2)
    return lax.dynamic_slice_in_dim(padded, (length - offset).astype(jnp.int32), length, values.ndim - 2)


def advanced(values, offset):
    length = values.shape[-2]
    padded = jnp.concatenate([values, jnp.zeros_like(values)], axis=-2)
    return lax.dynamic_slice_in_dim(padded, offset.astype(jnp.int32), length, values.ndim - 2)


def one_section(operands):
    saved, received, earlier, weight, taps_table, spacing = operands
    inputs = saved.astype(jnp.float32)
    conv = jnp.zeros(inputs.shape, jnp.float32)
    for tap in range(TAPS):
        conv = conv + taps_table[tap] * delayed(inputs, tap * spacing)
    hidden = conv.astype(jnp.bfloat16)
    back = jnp.dot(received, weight.T, preferred_element_type=jnp.float32)
    adjoint = received.astype(jnp.float32)
    for tap in range(TAPS):
        adjoint = adjoint + taps_table[tap] * advanced(back, tap * spacing)
    grad_input = adjoint.astype(jnp.bfloat16)
    grad_kernel = jnp.stack([jnp.sum(back * delayed(inputs[0], tap * spacing), axis=0) for tap in range(TAPS)])
    grad_weight = jnp.dot(hidden[0].T, received, preferred_element_type=jnp.float32)
    grad_weight = grad_weight + jnp.dot(hidden[1].T, earlier, preferred_element_type=jnp.float32)
    return grad_input, grad_kernel, grad_weight.astype(jnp.bfloat16)


def reference(saved_input, incoming, earlier_grad, w_out, kernel, dilation):
    received = jnp.roll(incoming, -1, axis=0)
    results = lax.map(one_section, (saved_input, received, earlier_grad, w_out, kernel, dilation))
    return (results[0], results[1], results[2])
```

```python
import functools

import jax
import jax.numpy as jnp
from jax import lax
from jax.experimental import pallas as pl
from jax.experimental.pallas import tpu as pltpu
from jax.sharding import PartitionSpec as P

TAPS = 3
SECTIONS = 16
NZ = 12
NY = 4
SEQ = 256
LANES = 128
VMEM_LIMIT = 48 * 1024 * 1024

BATCHES = ((0, -1, 1, -2, 2, -3, 3), (-4, 4, -5, 5, -6))


def along(block, move):
    route = []
    for i in range(NZ * NY):
        z, y = move(i // NY, i % NY)
        route.append((i, (z % NZ) * NY + y))
    return lax.ppermute(block, "fsdp", route)


def from_next_section(block, flip):
    total = NZ * NY
    route = []
    for s in range(SECTIONS):
        for i in range(total):
            source = ((s + 1) % SECTIONS) * total + (i ^ flip)
            route.append((source, s * total + i))
    return lax.ppermute(block, ("section", "fsdp"), route)


def delayed(values, offset):
    rows = lax.broadcasted_iota(jnp.int32, values.shape, 0)
    return jnp.where(rows >= offset, pltpu.roll(values, offset, 0), 0.0)


def advanced(values, offset):
    length = values.shape[0]
    rows = lax.broadcasted_iota(jnp.int32, values.shape, 0)
    shifted = pltpu.roll(values, lax.rem(length - offset, length), 0)
    return jnp.where(rows < length - offset, shifted, 0.0)


def hidden_kernel(spacing_ref, saved_ref, taps_ref, out_ref):
    spacing = spacing_ref[0]
    for slot, batch in ((0, 1), (1, 0)):
        values = saved_ref[batch].astype(jnp.float32)
        conv = taps_ref[0:1, :] * values
        for tap in range(1, TAPS):
            conv = conv + taps_ref[tap : tap + 1, :] * delayed(values, tap * spacing)
        out_ref[:, slot * SEQ : (slot + 1) * SEQ] = conv.T.astype(jnp.bfloat16)


def hidden_rows(saved, taps, spacing):
    return pl.pallas_call(
        hidden_kernel,
        out_shape=jax.ShapeDtypeStruct((LANES, 2 * SEQ), jnp.bfloat16),
        in_specs=[
            pl.BlockSpec(memory_space=pltpu.SMEM),
            pl.BlockSpec(memory_space=pltpu.VMEM),
            pl.BlockSpec(memory_space=pltpu.VMEM),
        ],
        out_specs=pl.BlockSpec(memory_space=pltpu.VMEM),
        compiler_params=pltpu.CompilerParams(vmem_limit_bytes=VMEM_LIMIT),
        name="hidden",
    )(spacing, saved, taps)


def split_kernel(place_ref, weight_ref, keep_ref, send_ref):
    y = place_ref[1]
    for z in range(weight_ref.shape[1] // (NY * LANES)):
        for slot, flip in ((0, 0), (1, 2)):
            for target, other in ((keep_ref, 0), (send_ref, 1)):
                column = (z * NY + (y ^ (flip + other))) * LANES
                target[slot, z] = weight_ref[:, pl.ds(pl.multiple_of(column, LANES), LANES)]


def split_weight(place, weight):
    steps, per = 3, NZ // 3
    out = jax.ShapeDtypeStruct((2, NZ, LANES, LANES), jnp.bfloat16)
    block = pl.BlockSpec((2, per, LANES, LANES), lambda i: (0, i, 0, 0))
    return pl.pallas_call(
        split_kernel,
        out_shape=(out, out),
        grid=(steps,),
        in_specs=[
            pl.BlockSpec(memory_space=pltpu.SMEM),
            pl.BlockSpec((LANES, per * NY * LANES), lambda i: (0, i)),
        ],
        out_specs=(block, block),
        compiler_params=pltpu.CompilerParams(vmem_limit_bytes=VMEM_LIMIT),
        name="split_weight",
    )(place, weight)


def partial_kernel(slot, places, place_ref, own_ref, partner_ref, keep_ref, got_ref, *refs):
    count = len(places)
    blocks = refs[:count] if count > 1 else [refs[0]]
    refs = refs[len(blocks) :]
    had_refs, (mine_ref, theirs_ref, back_mine_ref, back_theirs_ref) = refs[:-4], refs[-4:]
    left = jnp.concatenate([own_ref[...], partner_ref[...]], axis=0)
    if had_refs:
        back = jnp.concatenate([had_refs[0][...], had_refs[1][...]], axis=1)
    else:
        back = jnp.zeros((SEQ, 2 * LANES), jnp.float32)
    for i, place in enumerate(places):
        block = blocks[i][...]
        grad = jnp.dot(left, block, preferred_element_type=jnp.float32)
        mine_ref[i] = grad[:LANES].astype(jnp.bfloat16)
        theirs_ref[i] = grad[LANES:].astype(jnp.bfloat16)
        at = lax.rem(place_ref[0] + (place + NZ), NZ)
        weight = jnp.concatenate([keep_ref[slot, at], got_ref[slot, at]], axis=0)
        back = back + lax.dot_general(
            block[SEQ:], weight, (((1,), (1,)), ((), ())), preferred_element_type=jnp.float32
        )
    back_mine_ref[...] = back[:, :LANES]
    back_theirs_ref[...] = back[:, LANES:]


def gathered_kernel(place_ref, own_ref, partner_ref, keep_ref, got_ref, all_ref, had_mine, had_theirs, mine_ref, theirs_ref, back_mine_ref, back_theirs_ref):
    left = jnp.concatenate([own_ref[...], partner_ref[...]], axis=0)
    back = jnp.concatenate([had_mine[...], had_theirs[...]], axis=1)
    for z in range(NZ):
        block = all_ref[z]
        grad = jnp.dot(left, block, preferred_element_type=jnp.float32)
        mine_ref[z] = grad[:LANES].astype(jnp.bfloat16)
        theirs_ref[z] = grad[LANES:].astype(jnp.bfloat16)
        weight = jnp.concatenate([keep_ref[0, z], got_ref[0, z]], axis=0)
        back = back + lax.dot_general(
            block[SEQ:], weight, (((1,), (1,)), ((), ())), preferred_element_type=jnp.float32
        )
    back_mine_ref[...] = back[:, :LANES]
    back_theirs_ref[...] = back[:, LANES:]


def products(kernel, name, count, operands):
    grads = jax.ShapeDtypeStruct((count, LANES, LANES), jnp.bfloat16)
    backs = jax.ShapeDtypeStruct((SEQ, LANES), jnp.float32)
    flops = 2 * count * (2 * LANES * 2 * SEQ * LANES + SEQ * 2 * LANES * LANES)
    whole = pl.BlockSpec(memory_space=pltpu.VMEM)
    return pl.pallas_call(
        kernel,
        out_shape=(grads, grads, backs, backs),
        in_specs=[pl.BlockSpec(memory_space=pltpu.SMEM)] + [whole] * (len(operands) - 1),
        out_specs=(whole,) * 4,
        compiler_params=pltpu.CompilerParams(vmem_limit_bytes=VMEM_LIMIT),
        cost_estimate=pl.CostEstimate(flops=flops, bytes_accessed=1 << 20, transcendentals=0),
        name=name,
    )(*operands)


def adjoint_kernel(spacing_ref, received_ref, saved_ref, taps_ref, mine_ref, theirs_ref, input_ref, taps_out_ref):
    spacing = spacing_ref[0]
    back = mine_ref[...] + theirs_ref[...]
    values = saved_ref[0].astype(jnp.float32)
    total = received_ref[...].astype(jnp.float32)
    for tap in range(TAPS):
        offset = tap * spacing
        total = total + taps_ref[tap : tap + 1, :] * advanced(back, offset)
        taps_out_ref[tap : tap + 1, :] = jnp.sum(back * delayed(values, offset), axis=0, keepdims=True)
    input_ref[...] = total.astype(jnp.bfloat16)


def adjoint(spacing, received, saved, taps, mine, theirs):
    whole = pl.BlockSpec(memory_space=pltpu.VMEM)
    return pl.pallas_call(
        adjoint_kernel,
        out_shape=(
            jax.ShapeDtypeStruct((SEQ, LANES), jnp.bfloat16),
            jax.ShapeDtypeStruct((TAPS, LANES), jnp.float32),
        ),
        in_specs=[pl.BlockSpec(memory_space=pltpu.SMEM)] + [whole] * 5,
        out_specs=(whole, whole),
        compiler_params=pltpu.CompilerParams(vmem_limit_bytes=VMEM_LIMIT),
        name="adjoint",
    )(spacing, received, saved, taps, mine, theirs)


def assemble_kernel(place_ref, own_all_ref, got_all_ref, *refs):
    out_ref, refs = refs[-1], refs[:-1]
    z, y = place_ref[0], place_ref[1]
    for at in range(NZ):
        for flip, source in ((0, own_all_ref), (1, got_all_ref)):
            column = (at * NY + (y ^ flip)) * LANES
            out_ref[:, pl.ds(pl.multiple_of(column, LANES), LANES)] = source[at]
    for number, places in enumerate(BATCHES):
        for i, place in enumerate(places):
            at = lax.rem(z + (place + NZ), NZ)
            for flip, source in ((2, refs[2 * number]), (3, refs[2 * number + 1])):
                column = (at * NY + (y ^ flip)) * LANES
                out_ref[:, pl.ds(pl.multiple_of(column, LANES), LANES)] = source[i]


def assemble(place, own_all, got_all, pieces):
    whole = pl.BlockSpec(memory_space=pltpu.VMEM)
    return pl.pallas_call(
        assemble_kernel,
        out_shape=jax.ShapeDtypeStruct((LANES, NZ * NY * LANES), jnp.bfloat16),
        in_specs=[pl.BlockSpec(memory_space=pltpu.SMEM)] + [whole] * (2 + len(pieces)),
        out_specs=whole,
        compiler_params=pltpu.CompilerParams(vmem_limit_bytes=VMEM_LIMIT),
        name="assemble",
    )(place, own_all, got_all, *pieces)


def per_device(saved_input, incoming, earlier_grad, w_out, kernel, dilation):
    saved, taps, weight = saved_input[0], kernel[0], w_out[0]
    earlier = earlier_grad[0]
    index = lax.axis_index("fsdp")
    place = jnp.stack([index // NY, index % NY]).astype(jnp.int32)
    partner = lambda z, y: (z, y ^ 1)

    received = from_next_section(incoming[0], 0)
    received_other = from_next_section(incoming[0], 2)
    earlier_other = along(earlier, lambda z, y: (z, y ^ 2))
    own_block = jnp.concatenate([earlier, received], axis=0)
    groups = [[z * NY + y for z in range(NZ)] for y in range(NY)]
    gathered = lax.all_gather(own_block, "fsdp", axis=0, axis_index_groups=groups)

    ring = {0: jnp.concatenate([earlier_other, received_other], axis=0)}
    for step in range(1, NZ // 2 + 1):
        ring[-step] = along(ring[1 - step], lambda z, y: (z + 1, y))
        if step < NZ // 2:
            ring[step] = along(ring[step - 1], lambda z, y: (z - 1, y))

    rows = hidden_rows(saved, taps, dilation)
    rows_partner = along(rows, partner)
    keep, send = split_weight(place, weight)
    got = along(send, partner)

    backs, pieces = (), []
    for places in BATCHES:
        mine, theirs, *backs = products(
            functools.partial(partial_kernel, 1, places),
            "ring_products",
            len(places),
            (place, rows, rows_partner, keep, got, *(ring[p] for p in places), *backs),
        )
        pieces += [mine, along(theirs, partner)]
    own_all, theirs_all, back_mine, back_theirs = products(
        gathered_kernel, "gathered_products", NZ, (place, rows, rows_partner, keep, got, gathered, *backs)
    )
    back_other = along(back_theirs, partner)
    got_all = along(theirs_all, partner)
    grad_input, grad_kernel = adjoint(dilation, received, saved, taps, back_mine, back_other)
    grad_weight = assemble(place, own_all, got_all, pieces)
    return grad_input[None], grad_kernel[None], grad_weight[None]


def solution(mesh):
    return jax.shard_map(
        per_device,
        mesh=mesh,
        in_specs=(
            P("section", None, None, "fsdp"),
            P("section", None, "fsdp"),
            P("section", None, "fsdp"),
            P("section", "fsdp", None),
            P("section", None, "fsdp"),
            P("section"),
        ),
        out_specs=(
            P("section", None, "fsdp"),
            P("section", None, "fsdp"),
            P("section", "fsdp", None),
        ),
        check_vma=False,
    )
```

```python
import functools

import jax
import jax.numpy as jnp
from jax import lax
from jax.experimental import pallas as pl
from jax.experimental.pallas import tpu as pltpu
from jax.sharding import PartitionSpec as P

TAPS = 3
SECTIONS = 16
NZ = 12
NY = 4
SEQ = 256
LANES = 128
VMEM_LIMIT = 48 * 1024 * 1024

PAIR = 2 * LANES
BATCHES = ((0, -1, 1, -2, 2, -3, 3), (-4, 4, -5, 5), (-6,))


def along(block, move):
    route = []
    for i in range(NZ * NY):
        z, y = move(i // NY, i % NY)
        route.append((i, (z % NZ) * NY + y))
    return lax.ppermute(block, "fsdp", route)


def from_next_section(block, flip):
    total = NZ * NY
    route = []
    for s in range(SECTIONS):
        for i in range(total):
            source = ((s + 1) % SECTIONS) * total + (i ^ flip)
            route.append((source, s * total + i))
    return lax.ppermute(block, ("section", "fsdp"), route)


def delayed(values, offset):
    rows = lax.broadcasted_iota(jnp.int32, values.shape, 0)
    return jnp.where(rows >= offset, pltpu.roll(values, offset, 0), 0.0)


def advanced(values, offset):
    length = values.shape[0]
    rows = lax.broadcasted_iota(jnp.int32, values.shape, 0)
    shifted = pltpu.roll(values, lax.rem(length - offset, length), 0)
    return jnp.where(rows < length - offset, shifted, 0.0)


def hidden_kernel(spacing_ref, saved_ref, taps_ref, out_ref):
    spacing = spacing_ref[0]
    for slot, batch in ((0, 1), (1, 0)):
        values = saved_ref[batch].astype(jnp.float32)
        conv = taps_ref[0:1, :] * values
        for tap in range(1, TAPS):
            conv = conv + taps_ref[tap : tap + 1, :] * delayed(values, tap * spacing)
        out_ref[:, slot * SEQ : (slot + 1) * SEQ] = conv.T.astype(jnp.bfloat16)


def hidden_rows(saved, taps, spacing):
    return pl.pallas_call(
        hidden_kernel,
        out_shape=jax.ShapeDtypeStruct((LANES, 2 * SEQ), jnp.bfloat16),
        in_specs=[
            pl.BlockSpec(memory_space=pltpu.SMEM),
            pl.BlockSpec(memory_space=pltpu.VMEM),
            pl.BlockSpec(memory_space=pltpu.VMEM),
        ],
        out_specs=pl.BlockSpec(memory_space=pltpu.VMEM),
        compiler_params=pltpu.CompilerParams(vmem_limit_bytes=VMEM_LIMIT),
        name="hidden",
    )(spacing, saved, taps)


def pack_kernel(*refs):
    for i in range(4):
        row, column = (i // 2) * SEQ, (i % 2) * LANES
        refs[4][row : row + SEQ, column : column + LANES] = refs[i][...]


def pack(earlier, earlier_other, received, received_other):
    whole = pl.BlockSpec(memory_space=pltpu.VMEM)
    return pl.pallas_call(
        pack_kernel,
        out_shape=jax.ShapeDtypeStruct((2 * SEQ, PAIR), jnp.bfloat16),
        in_specs=[whole] * 4,
        out_specs=whole,
        compiler_params=pltpu.CompilerParams(vmem_limit_bytes=VMEM_LIMIT),
        name="pack",
    )(earlier, earlier_other, received, received_other)


def columns_of(z, y):
    return pl.ds(pl.multiple_of((z * NY + y) * LANES, LANES), LANES)


def split_kernel(place_ref, weight_ref, keep_ref, send_ref):
    y = place_ref[1]
    for z in range(weight_ref.shape[1] // (NY * LANES)):
        for flip, lanes in ((0, slice(0, LANES)), (2, slice(LANES, PAIR))):
            keep_ref[z, :, lanes] = weight_ref[:, columns_of(z, y ^ flip)]
            send_ref[z, :, lanes] = weight_ref[:, columns_of(z, y ^ (flip + 1))]


def split_weight(place, weight):
    steps, per = 3, NZ // 3
    out = jax.ShapeDtypeStruct((NZ, LANES, PAIR), jnp.bfloat16)
    block = pl.BlockSpec((per, LANES, PAIR), lambda i: (i, 0, 0))
    return pl.pallas_call(
        split_kernel,
        out_shape=(out, out),
        grid=(steps,),
        in_specs=[
            pl.BlockSpec(memory_space=pltpu.SMEM),
            pl.BlockSpec((LANES, per * NY * LANES), lambda i: (0, i)),
        ],
        out_specs=(block, block),
        compiler_params=pltpu.CompilerParams(vmem_limit_bytes=VMEM_LIMIT),
        name="split_weight",
    )(place, weight)


def products_kernel(places, place_ref, own_ref, partner_ref, keep_ref, got_ref, *refs):
    blocks, refs = refs[: len(places)], refs[len(places) :]
    had_refs, (mine_ref, theirs_ref, back_mine_ref, back_theirs_ref) = refs[:-4], refs[-4:]
    left = jnp.concatenate([own_ref[...], partner_ref[...]], axis=0)
    if had_refs:
        back = jnp.concatenate([had_refs[0][...], had_refs[1][...]], axis=1)
    else:
        back = jnp.zeros((SEQ, PAIR), jnp.float32)
    for i, place in enumerate(places):
        block = blocks[i][...]
        grad = jnp.dot(left, block, preferred_element_type=jnp.float32)
        mine_ref[i] = grad[:LANES].astype(jnp.bfloat16)
        theirs_ref[i] = grad[LANES:].astype(jnp.bfloat16)
        at = lax.rem(place_ref[0] + (place + NZ), NZ)
        weight = jnp.concatenate([keep_ref[at], got_ref[at]], axis=0)
        back = back + lax.dot_general(
            block[SEQ:], weight, (((1,), (1,)), ((), ())), preferred_element_type=jnp.float32
        )
    back_mine_ref[...] = back[:, :LANES]
    back_theirs_ref[...] = back[:, LANES:]


def products(places, operands):
    count = len(places)
    grads = jax.ShapeDtypeStruct((count, LANES, PAIR), jnp.bfloat16)
    backs = jax.ShapeDtypeStruct((SEQ, LANES), jnp.float32)
    flops = 4 * count * PAIR * 2 * SEQ * PAIR
    whole = pl.BlockSpec(memory_space=pltpu.VMEM)
    return pl.pallas_call(
        functools.partial(products_kernel, places),
        out_shape=(grads, grads, backs, backs),
        in_specs=[pl.BlockSpec(memory_space=pltpu.SMEM)] + [whole] * (len(operands) - 1),
        out_specs=(whole,) * 4,
        compiler_params=pltpu.CompilerParams(vmem_limit_bytes=VMEM_LIMIT),
        cost_estimate=pl.CostEstimate(flops=flops, bytes_accessed=1 << 20, transcendentals=0),
        name="products",
    )(*operands)


def adjoint_kernel(spacing_ref, received_ref, saved_ref, taps_ref, mine_ref, theirs_ref, input_ref, taps_out_ref):
    spacing = spacing_ref[0]
    back = mine_ref[...] + theirs_ref[...]
    values = saved_ref[0].astype(jnp.float32)
    total = received_ref[...].astype(jnp.float32)
    for tap in range(TAPS):
        offset = tap * spacing
        total = total + taps_ref[tap : tap + 1, :] * advanced(back, offset)
        taps_out_ref[tap : tap + 1, :] = jnp.sum(back * delayed(values, offset), axis=0, keepdims=True)
    input_ref[...] = total.astype(jnp.bfloat16)


def adjoint(spacing, received, saved, taps, mine, theirs):
    whole = pl.BlockSpec(memory_space=pltpu.VMEM)
    return pl.pallas_call(
        adjoint_kernel,
        out_shape=(
            jax.ShapeDtypeStruct((SEQ, LANES), jnp.bfloat16),
            jax.ShapeDtypeStruct((TAPS, LANES), jnp.float32),
        ),
        in_specs=[pl.BlockSpec(memory_space=pltpu.SMEM)] + [whole] * 5,
        out_specs=(whole, whole),
        compiler_params=pltpu.CompilerParams(vmem_limit_bytes=VMEM_LIMIT),
        name="adjoint",
    )(spacing, received, saved, taps, mine, theirs)


def put(out_ref, z, y, source, flip):
    out_ref[:, columns_of(z, y ^ flip)] = source[:, :LANES]
    out_ref[:, columns_of(z, y ^ (flip + 2))] = source[:, LANES:]


def assemble_kernel(batches, place_ref, *refs):
    out_ref = refs[-1]
    for number, places in enumerate(batches):
        for i, place in enumerate(places):
            at = lax.rem(place_ref[0] + (place + NZ), NZ)
            put(out_ref, at, place_ref[1], refs[2 * number][i], 0)
            put(out_ref, at, place_ref[1], refs[2 * number + 1][i], 1)


def assemble(place, batches, pieces):
    whole = pl.BlockSpec(memory_space=pltpu.VMEM)
    return pl.pallas_call(
        functools.partial(assemble_kernel, batches),
        out_shape=jax.ShapeDtypeStruct((LANES, NZ * NY * LANES), jnp.bfloat16),
        in_specs=[pl.BlockSpec(memory_space=pltpu.SMEM)] + [whole] * len(pieces),
        out_specs=whole,
        compiler_params=pltpu.CompilerParams(vmem_limit_bytes=VMEM_LIMIT),
        name="assemble",
    )(place, *pieces)


def finish_kernel(place_ref, mine_ref, got_ref, whole_ref, out_ref):
    put(out_ref, 0, place_ref[1], mine_ref[0], 0)
    put(out_ref, 0, place_ref[1], got_ref[0], 1)


def finish(place, mine, got, whole):
    piece = pl.BlockSpec((1, LANES, PAIR), lambda i, place: (0, 0, 0))
    return pl.pallas_call(
        finish_kernel,
        out_shape=jax.ShapeDtypeStruct(whole.shape, whole.dtype),
        grid_spec=pltpu.PrefetchScalarGridSpec(
            num_scalar_prefetch=1,
            grid=(1,),
            in_specs=[piece, piece, pl.BlockSpec(memory_space=pl.ANY)],
            out_specs=pl.BlockSpec((LANES, NY * LANES), lambda i, place: (0, lax.rem(place[0] + NZ // 2, NZ))),
        ),
        input_output_aliases={3: 0},
        name="finish",
    )(place, mine, got, whole)


def per_device(saved_input, incoming, earlier_grad, w_out, kernel, dilation):
    saved, taps, weight = saved_input[0], kernel[0], w_out[0]
    earlier = earlier_grad[0]
    index = lax.axis_index("fsdp")
    place = jnp.stack([lax.div(index, NY), lax.rem(index, NY)]).astype(jnp.int32)
    partner = lambda z, y: (z, y ^ 1)

    received = from_next_section(incoming[0], 0)
    received_other = from_next_section(incoming[0], 2)
    earlier_other = along(earlier, lambda z, y: (z, y ^ 2))
    ring = {0: pack(earlier, earlier_other, received, received_other)}
    for step in range(1, NZ // 2 + 1):
        ring[-step] = along(ring[1 - step], lambda z, y: (z + 1, y))
        if step < NZ // 2:
            ring[step] = along(ring[step - 1], lambda z, y: (z - 1, y))

    rows = hidden_rows(saved, taps, dilation)
    rows_partner = along(rows, partner)
    keep, send = split_weight(place, weight)
    got = along(send, partner)

    backs, pieces = (), []
    for places in BATCHES:
        mine, theirs, *backs = products(places, (place, rows, rows_partner, keep, got, *(ring[p] for p in places), *backs))
        if places == BATCHES[-1]:
            back_other = along(backs[1], partner)
        pieces += [mine, along(theirs, partner)]
    grad_input, grad_kernel = adjoint(dilation, received, saved, taps, backs[0], back_other)
    grad_weight = finish(place, *pieces[-2:], assemble(place, BATCHES[:-1], pieces[:-2]))
    return grad_input[None], grad_kernel[None], grad_weight[None]


def solution(mesh):
    return jax.shard_map(
        per_device,
        mesh=mesh,
        in_specs=(
            P("section", None, None, "fsdp"),
            P("section", None, "fsdp"),
            P("section", None, "fsdp"),
            P("section", "fsdp", None),
            P("section", None, "fsdp"),
            P("section"),
        ),
        out_specs=(
            P("section", None, "fsdp"),
            P("section", None, "fsdp"),
            P("section", "fsdp", None),
        ),
        check_vma=False,
    )
```

```python
import functools

import jax
import jax.numpy as jnp
from jax import lax
from jax.experimental import pallas as pl
from jax.experimental.pallas import tpu as pltpu
from jax.sharding import PartitionSpec as P

TAPS = 3
SECTIONS = 16
NZ = 12
NY = 4
SEQ = 256
LANES = 128
VMEM_LIMIT = 48 * 1024 * 1024

PAIR = 2 * LANES
EARLY = ((0, -1, 1, -2, 2, -3, 3), (-4, 4, -5, 5))
LAST = (-6,)
EXTRA = 2


def along(block, move):
    route = []
    for i in range(NZ * NY):
        z, y = move(i // NY, i % NY)
        route.append((i, (z % NZ) * NY + y))
    return lax.ppermute(block, "fsdp", route)


def from_next_section(block, flip):
    total = NZ * NY
    route = []
    for s in range(SECTIONS):
        for i in range(total):
            source = ((s + 1) % SECTIONS) * total + (i ^ flip)
            route.append((source, s * total + i))
    return lax.ppermute(block, ("section", "fsdp"), route)


def delayed(values, offset):
    rows = lax.broadcasted_iota(jnp.int32, values.shape, 0)
    return jnp.where(rows >= offset, pltpu.roll(values, offset, 0), 0.0)


def advanced(values, offset):
    length = values.shape[0]
    rows = lax.broadcasted_iota(jnp.int32, values.shape, 0)
    shifted = pltpu.roll(values, lax.rem(length - offset, length), 0)
    return jnp.where(rows < length - offset, shifted, 0.0)


def pack_kernel(*refs):
    for i in range(4):
        row, column = (i // 2) * SEQ, (i % 2) * LANES
        refs[4][row : row + SEQ, column : column + LANES] = refs[i][...]


def pack(earlier, earlier_other, received, received_other):
    whole = pl.BlockSpec(memory_space=pltpu.VMEM)
    return pl.pallas_call(
        pack_kernel,
        out_shape=jax.ShapeDtypeStruct((2 * SEQ, PAIR), jnp.bfloat16),
        in_specs=[whole] * 4,
        out_specs=whole,
        compiler_params=pltpu.CompilerParams(vmem_limit_bytes=VMEM_LIMIT),
        name="pack",
    )(earlier, earlier_other, received, received_other)


def columns_of(z, y):
    return pl.ds(pl.multiple_of((z * NY + y) * LANES, LANES), LANES)


def prepare_kernel(place_ref, spacing_ref, saved_ref, taps_ref, weight_ref, keep_ref, send_ref):
    y, spacing = place_ref[1], spacing_ref[0]
    for slot, batch in ((0, 1), (1, 0)):
        values = saved_ref[batch].astype(jnp.float32)
        conv = taps_ref[0, 0:1, :] * values
        for tap in range(1, TAPS):
            conv = conv + taps_ref[0, tap : tap + 1, :] * delayed(values, tap * spacing)
        rows = conv.T.astype(jnp.bfloat16)
        keep_ref[NZ + slot] = rows
        send_ref[NZ + slot] = rows
    for z in range(NZ):
        for flip, lanes in ((0, slice(0, LANES)), (2, slice(LANES, PAIR))):
            keep_ref[z, :, lanes] = weight_ref[:, columns_of(z, y ^ flip)]
            send_ref[z, :, lanes] = weight_ref[:, columns_of(z, y ^ (flip + 1))]


def prepare(place, spacing, saved, taps, weight):
    out = jax.ShapeDtypeStruct((NZ + EXTRA, LANES, PAIR), jnp.bfloat16)
    return call(prepare_kernel, "prepare", (out, out), (place, spacing), (saved, taps, weight))


def call(kernel, name, outs, scalars, arrays, flops=0):
    whole, scalar = pl.BlockSpec(memory_space=pltpu.VMEM), pl.BlockSpec(memory_space=pltpu.SMEM)
    return pl.pallas_call(
        kernel,
        out_shape=outs,
        in_specs=[scalar] * len(scalars) + [whole] * len(arrays),
        out_specs=(whole,) * len(outs),
        compiler_params=pltpu.CompilerParams(vmem_limit_bytes=VMEM_LIMIT),
        cost_estimate=pl.CostEstimate(flops=flops, bytes_accessed=1 << 20, transcendentals=0),
        name=name,
    )(*scalars, *arrays)


def products_kernel(places, last, place_ref, keep_ref, got_ref, *refs):
    blocks, refs = refs[: len(places)], refs[len(places) :]
    had_refs, (mine_ref, theirs_ref, back_ref) = refs[:-3], refs[-3:]
    left = jnp.concatenate(
        [jnp.concatenate([ref[NZ], ref[NZ + 1]], axis=1) for ref in (keep_ref, got_ref)], axis=0
    )
    back = had_refs[0][...] if had_refs else jnp.zeros((SEQ, PAIR), jnp.float32)
    for i, place in enumerate(places):
        block = blocks[i][...]
        grad = jnp.dot(left, block, preferred_element_type=jnp.float32)
        mine_ref[i] = grad[:LANES].astype(jnp.bfloat16)
        theirs_ref[i] = grad[LANES:].astype(jnp.bfloat16)
        at = lax.rem(place_ref[0] + (place + NZ), NZ)
        weight = jnp.concatenate([keep_ref[at], got_ref[at]], axis=0)
        back = back + lax.dot_general(
            block[SEQ:], weight, (((1,), (1,)), ((), ())), preferred_element_type=jnp.float32
        )
    if last:
        other = back[:, LANES:]
        high = other.astype(jnp.bfloat16)
        low = (other - high.astype(jnp.float32)).astype(jnp.bfloat16)
        for i, part in enumerate((high, low)):
            theirs_ref[len(places) + i] = jnp.concatenate([part[:LANES], part[LANES:]], axis=1)
        back_ref[...] = back[:, :LANES]
    else:
        back_ref[...] = back


def products(places, last, place, arrays):
    count = len(places)
    outs = (
        jax.ShapeDtypeStruct((count, LANES, PAIR), jnp.bfloat16),
        jax.ShapeDtypeStruct((count + (EXTRA if last else 0), LANES, PAIR), jnp.bfloat16),
        jax.ShapeDtypeStruct((SEQ, LANES if last else PAIR), jnp.float32),
    )
    flops = 4 * count * PAIR * 2 * SEQ * PAIR
    return call(functools.partial(products_kernel, places, last), "products", outs, (place,), arrays, flops)


def put(out_ref, z, y, source, flip):
    out_ref[:, columns_of(z, y ^ flip)] = source[:, :LANES]
    out_ref[:, columns_of(z, y ^ (flip + 2))] = source[:, LANES:]


def finish_kernel(place_ref, spacing_ref, received_ref, saved_ref, taps_ref, back_ref, *refs):
    pieces, (input_ref, taps_out_ref, out_ref) = refs[:-3], refs[-3:]
    z, y, spacing = place_ref[0], place_ref[1], spacing_ref[0]
    last = pieces[-1]
    parts = [last[len(LAST) + i].astype(jnp.float32) for i in range(EXTRA)]
    total = parts[0] + parts[1]
    back = back_ref[...] + jnp.concatenate([total[:, :LANES], total[:, LANES:]], axis=0)
    values = saved_ref[0].astype(jnp.float32)
    adjoint = received_ref[...].astype(jnp.float32)
    for tap in range(TAPS):
        offset = tap * spacing
        adjoint = adjoint + taps_ref[0, tap : tap + 1, :] * advanced(back, offset)
        taps_out_ref[0, tap : tap + 1, :] = jnp.sum(back * delayed(values, offset), axis=0, keepdims=True)
    input_ref[...] = adjoint.astype(jnp.bfloat16)
    for number, places in enumerate((*EARLY, LAST)):
        for i, place in enumerate(places):
            at = lax.rem(z + (place + NZ), NZ)
            put(out_ref, at, y, pieces[number][i], 0)
            put(out_ref, at, y, pieces[len(EARLY) + 1 + number][i], 1)


def per_device(saved_input, incoming, earlier_grad, w_out, kernel, dilation):
    saved, weight = saved_input[0], w_out[0]
    earlier = earlier_grad[0]
    index = lax.axis_index("fsdp")
    place = jnp.stack([lax.div(index, NY), lax.rem(index, NY)]).astype(jnp.int32)
    partner = lambda z, y: (z, y ^ 1)

    received = from_next_section(incoming[0], 0)
    received_other = from_next_section(incoming[0], 2)
    earlier_other = along(earlier, lambda z, y: (z, y ^ 2))
    keep, send = prepare(place, dilation, saved, kernel, weight)
    ring, back, mine, other = {0: pack(earlier, earlier_other, received, received_other)}, (), [], []
    for step in range(1, NZ // 2 + 1):
        if step == 2:
            ring[-1], ring[1], keep, send = lax.optimization_barrier((ring[-1], ring[1], keep, send))
            got = along(send, partner)
        if step == 5:
            one, two, *back = products(EARLY[0], False, place, (keep, got, *(ring[p] for p in EARLY[0])))
            mine.append(one)
            ring[1 - step], two = lax.optimization_barrier((ring[1 - step], two))
            other.append(along(two, partner))
        ring[-step] = along(ring[1 - step], lambda z, y: (z + 1, y))
        if step < NZ // 2:
            ring[step] = along(ring[step - 1], lambda z, y: (z - 1, y))
    one, two, *back = products(EARLY[1], False, place, (keep, got, *(ring[p] for p in EARLY[1]), *back))
    mine.append(one)
    other.append(along(two, partner))
    ring[LAST[0]], other[0] = lax.optimization_barrier((ring[LAST[0]], other[0]))
    one, two, back = products(LAST, True, place, (keep, got, *(ring[p] for p in LAST), *back))
    mine.append(one)
    other.append(along(two, partner))
    outs = (
        jax.ShapeDtypeStruct((SEQ, LANES), jnp.bfloat16),
        jax.ShapeDtypeStruct((1, TAPS, LANES), jnp.float32),
        jax.ShapeDtypeStruct((LANES, NZ * NY * LANES), jnp.bfloat16),
    )
    grad_input, grad_kernel, grad_weight = call(
        finish_kernel, "finish", outs, (place, dilation), (received, saved, kernel, back, *mine, *other)
    )
    return grad_input[None], grad_kernel, grad_weight[None]


def solution(mesh):
    return jax.shard_map(
        per_device,
        mesh=mesh,
        in_specs=(
            P("section", None, None, "fsdp"),
            P("section", None, "fsdp"),
            P("section", None, "fsdp"),
            P("section", "fsdp", None),
            P("section", None, "fsdp"),
            P("section"),
        ),
        out_specs=(
            P("section", None, "fsdp"),
            P("section", None, "fsdp"),
            P("section", "fsdp", None),
        ),
        check_vma=False,
    )
```

```python
import functools

import jax
import jax.numpy as jnp
from jax import lax
from jax.experimental import pallas as pl
from jax.experimental.pallas import tpu as pltpu
from jax.sharding import PartitionSpec as P

TAPS = 3
SECTIONS = 16
NZ = 12
NY = 4
SEQ = 256
LANES = 128
VMEM_LIMIT = 48 * 1024 * 1024

PAIR = 2 * LANES
EARLY = ((0, -1, 1, -2, 2, -3, 3), (-4, 4, -5, 5))
LAST = (-6,)
EXTRA = 2


def along(block, move):
    route = []
    for i in range(NZ * NY):
        z, y = move(i // NY, i % NY)
        route.append((i, (z % NZ) * NY + y))
    return lax.ppermute(block, "fsdp", route)


def from_next_section(block, flip):
    total = NZ * NY
    route = []
    for s in range(SECTIONS):
        for i in range(total):
            source = ((s + 1) % SECTIONS) * total + (i ^ flip)
            route.append((source, s * total + i))
    return lax.ppermute(block, ("section", "fsdp"), route)


def delayed(values, offset):
    rows = lax.broadcasted_iota(jnp.int32, values.shape, 0)
    return jnp.where(rows >= offset, pltpu.roll(values, offset, 0), 0.0)


def advanced(values, offset):
    length = values.shape[0]
    rows = lax.broadcasted_iota(jnp.int32, values.shape, 0)
    shifted = pltpu.roll(values, lax.rem(length - offset, length), 0)
    return jnp.where(rows < length - offset, shifted, 0.0)


def pack_kernel(*refs):
    for i in range(4):
        row, column = (i // 2) * SEQ, (i % 2) * LANES
        refs[4][row : row + SEQ, column : column + LANES] = refs[i][...]


def pack(earlier, earlier_other, received, received_other):
    whole = pl.BlockSpec(memory_space=pltpu.VMEM)
    return pl.pallas_call(
        pack_kernel,
        out_shape=jax.ShapeDtypeStruct((2 * SEQ, PAIR), jnp.bfloat16),
        in_specs=[whole] * 4,
        out_specs=whole,
        compiler_params=pltpu.CompilerParams(vmem_limit_bytes=VMEM_LIMIT),
        name="pack",
    )(earlier, earlier_other, received, received_other)


def columns_of(z, y):
    return pl.ds(pl.multiple_of((z * NY + y) * LANES, LANES), LANES)


def prepare_kernel(place_ref, spacing_ref, saved_ref, taps_ref, weight_ref, keep_ref, send_ref):
    y, spacing = place_ref[1], spacing_ref[0]
    for slot, batch in ((0, 1), (1, 0)):
        values = saved_ref[batch].astype(jnp.float32)
        conv = taps_ref[0, 0:1, :] * values
        for tap in range(1, TAPS):
            conv = conv + taps_ref[0, tap : tap + 1, :] * delayed(values, tap * spacing)
        rows = conv.T.astype(jnp.bfloat16)
        keep_ref[NZ + slot] = rows
        send_ref[NZ + slot] = rows
    for z in range(NZ):
        for flip, lanes in ((0, slice(0, LANES)), (2, slice(LANES, PAIR))):
            keep_ref[z, :, lanes] = weight_ref[:, columns_of(z, y ^ flip)]
            send_ref[z, :, lanes] = weight_ref[:, columns_of(z, y ^ (flip + 1))]


def prepare(place, spacing, saved, taps, weight):
    out = jax.ShapeDtypeStruct((NZ + EXTRA, LANES, PAIR), jnp.bfloat16)
    return call(prepare_kernel, "prepare", (out, out), (place, spacing), (saved, taps, weight))


def call(kernel, name, outs, scalars, arrays, flops=0):
    whole, scalar = pl.BlockSpec(memory_space=pltpu.VMEM), pl.BlockSpec(memory_space=pltpu.SMEM)
    return pl.pallas_call(
        kernel,
        out_shape=outs,
        in_specs=[scalar] * len(scalars) + [whole] * len(arrays),
        out_specs=(whole,) * len(outs),
        compiler_params=pltpu.CompilerParams(vmem_limit_bytes=VMEM_LIMIT),
        cost_estimate=pl.CostEstimate(flops=flops, bytes_accessed=1 << 20, transcendentals=0),
        name=name,
    )(*scalars, *arrays)


def products_kernel(places, last, place_ref, keep_ref, got_ref, *refs):
    blocks, refs = refs[: len(places)], refs[len(places) :]
    had_refs, (mine_ref, theirs_ref, back_ref) = refs[:-3], refs[-3:]
    left = jnp.concatenate(
        [jnp.concatenate([ref[NZ], ref[NZ + 1]], axis=1) for ref in (keep_ref, got_ref)], axis=0
    )
    back = had_refs[0][...] if had_refs else jnp.zeros((SEQ, PAIR), jnp.float32)
    for i, place in enumerate(places):
        block = blocks[i][...]
        grad = jnp.dot(left, block, preferred_element_type=jnp.float32)
        mine_ref[i] = grad[:LANES].astype(jnp.bfloat16)
        theirs_ref[i] = grad[LANES:].astype(jnp.bfloat16)
        at = lax.rem(place_ref[0] + (place + NZ), NZ)
        weight = jnp.concatenate([keep_ref[at], got_ref[at]], axis=0)
        back = back + lax.dot_general(
            block[SEQ:], weight, (((1,), (1,)), ((), ())), preferred_element_type=jnp.float32
        )
    if last:
        other = back[:, LANES:]
        high = other.astype(jnp.bfloat16)
        low = (other - high.astype(jnp.float32)).astype(jnp.bfloat16)
        for i, part in enumerate((high, low)):
            theirs_ref[len(places) + i] = jnp.concatenate([part[:LANES], part[LANES:]], axis=1)
        back_ref[...] = back[:, :LANES]
    else:
        back_ref[...] = back


def products(places, last, place, arrays):
    count = len(places)
    outs = (
        jax.ShapeDtypeStruct((count, LANES, PAIR), jnp.bfloat16),
        jax.ShapeDtypeStruct((count + (EXTRA if last else 0), LANES, PAIR), jnp.bfloat16),
        jax.ShapeDtypeStruct((SEQ, LANES if last else PAIR), jnp.float32),
    )
    flops = 4 * count * PAIR * 2 * SEQ * PAIR
    return call(functools.partial(products_kernel, places, last), "products", outs, (place,), arrays, flops)


def put(out_ref, z, y, source, flip):
    out_ref[:, columns_of(z, y ^ flip)] = source[:, :LANES]
    out_ref[:, columns_of(z, y ^ (flip + 2))] = source[:, LANES:]


def finish_kernel(place_ref, spacing_ref, received_ref, saved_ref, taps_ref, back_ref, *refs):
    pieces, (input_ref, taps_out_ref, out_ref) = refs[:-3], refs[-3:]
    z, y, spacing = place_ref[0], place_ref[1], spacing_ref[0]
    last = pieces[-1]
    parts = [last[len(LAST) + i].astype(jnp.float32) for i in range(EXTRA)]
    total = parts[0] + parts[1]
    back = back_ref[...] + jnp.concatenate([total[:, :LANES], total[:, LANES:]], axis=0)
    values = saved_ref[0].astype(jnp.float32)
    adjoint = received_ref[...].astype(jnp.float32)
    for tap in range(TAPS):
        offset = tap * spacing
        adjoint = adjoint + taps_ref[0, tap : tap + 1, :] * advanced(back, offset)
        taps_out_ref[0, tap : tap + 1, :] = jnp.sum(back * delayed(values, offset), axis=0, keepdims=True)
    input_ref[...] = adjoint.astype(jnp.bfloat16)
    for number, places in enumerate((*EARLY, LAST)):
        for i, place in enumerate(places):
            at = lax.rem(z + (place + NZ), NZ)
            put(out_ref, at, y, pieces[number][i], 0)
            put(out_ref, at, y, pieces[len(EARLY) + 1 + number][i], 1)


def per_device(saved_input, incoming, earlier_grad, w_out, kernel, dilation):
    saved, weight = saved_input[0], w_out[0]
    earlier = earlier_grad[0]
    index = lax.axis_index("fsdp")
    place = jnp.stack([lax.div(index, NY), lax.rem(index, NY)]).astype(jnp.int32)
    partner = lambda z, y: (z, y ^ 1)

    received = from_next_section(incoming[0], 0)
    received_other = from_next_section(incoming[0], 2)
    earlier_other = along(earlier, lambda z, y: (z, y ^ 2))
    keep, send = prepare(place, dilation, saved, kernel, weight)
    ring, back, mine, other = {0: pack(earlier, earlier_other, received, received_other)}, (), [], []
    for step in range(1, NZ // 2 + 1):
        if step == 2:
            ring[1], keep, send = lax.optimization_barrier((ring[1], keep, send))
            got = along(send, partner)
        if step == 5:
            one, two, *back = products(EARLY[0], False, place, (keep, got, *(ring[p] for p in EARLY[0])))
            mine.append(one)
            ring[1 - step], two = lax.optimization_barrier((ring[1 - step], two))
            other.append(along(two, partner))
        ring[-step] = along(ring[1 - step], lambda z, y: (z + 1, y))
        if step < NZ // 2:
            ring[step] = along(ring[step - 1], lambda z, y: (z - 1, y))
    one, two, *back = products(EARLY[1], False, place, (keep, got, *(ring[p] for p in EARLY[1]), *back))
    mine.append(one)
    other.append(along(two, partner))
    ring[LAST[0]], other[0] = lax.optimization_barrier((ring[LAST[0]], other[0]))
    one, two, back = products(LAST, True, place, (keep, got, *(ring[p] for p in LAST), *back))
    mine.append(one)
    other.append(along(two, partner))
    outs = (
        jax.ShapeDtypeStruct((SEQ, LANES), jnp.bfloat16),
        jax.ShapeDtypeStruct((1, TAPS, LANES), jnp.float32),
        jax.ShapeDtypeStruct((LANES, NZ * NY * LANES), jnp.bfloat16),
    )
    grad_input, grad_kernel, grad_weight = call(
        finish_kernel, "finish", outs, (place, dilation), (received, saved, kernel, back, *mine, *other)
    )
    return grad_input[None], grad_kernel, grad_weight[None]


def solution(mesh):
    return jax.shard_map(
        per_device,
        mesh=mesh,
        in_specs=(
            P("section", None, None, "fsdp"),
            P("section", None, "fsdp"),
            P("section", None, "fsdp"),
            P("section", "fsdp", None),
            P("section", None, "fsdp"),
            P("section"),
        ),
        out_specs=(
            P("section", None, "fsdp"),
            P("section", None, "fsdp"),
            P("section", "fsdp", None),
        ),
        check_vma=False,
    )
```
